512 devices in a mesh: dp: 32 (over z, y_lo), tensor: 16 (over x, y_hi, core).
Axes of the slice: x: 4, y: 4 (y_hi: 2, y_lo: 2; y = y_hi * 2 + y_lo), z: 16, core: 2. Of those that a mesh axis runs over, the one named last changes fastest.
Arguments:
- master: float32 [4096, 4096], P('dp', 'tensor'), may hold values from -36 to 36
- grad: float32 [4096, 4096], P('dp', 'tensor'), may hold values from -6 to 6
- moment: float32 [4096, 4096], P('dp', 'tensor'), may hold values from -4 to 4
- second: float32 [4096, 4096], P('dp', 'tensor'), may hold values from 0.1 to 2
Outputs:
- new_master: float32 [4096, 4096], P('dp', 'tensor')
- new_moment: float32 [4096, 4096], P('dp', 'tensor')
- new_second: float32 [4096, 4096], P('dp', 'tensor')
- block_scales: float32 [32, 32], P('dp', 'tensor')
- forward_copy: bfloat16 [4096, 4096], P('dp')
- transposed_copy: bfloat16 [16, 256, 4096], P(None, 'dp')
The draws below stay inside these ranges and needn't reach their ends.
All inputs are finite; a program needn't handle non-finite values. Where the reference program divides by a largest or mean magnitude, that divisor is 1e-20 or more.
Results may differ from the reference program's by a relative error of at most 0.001.
Values may be sent and summed in bfloat16 or wider, within the bound.
No kernel may reach another device: no remote copies, remote signals or barrier semaphores. Data moves between devices by JAX's collectives and lax.ppermute only.
A program may use at most 64 MiB of HBM per device.

```python
import math
import jax
import jax.numpy as jnp
from jax import lax

ROWS = 4096
COLS = 4096
BLOCK = 128
N_TENSOR = 16


def draw_master(key, part):
    key = jax.random.fold_in(key, 11)
    first, rowkey, colkey = jax.random.split(key, 3)
    base = jnp.clip(jax.random.normal(first, (ROWS, COLS), jnp.float32), -4.0, 4.0)
    lower, upper = (math.log(0.3), math.log(3.0))
    row_scale = jnp.exp(jax.random.uniform(rowkey, (ROWS, 1), jnp.float32, lower, upper))
    col_scale = jnp.exp(jax.random.uniform(colkey, (1, COLS), jnp.float32, lower, upper))
    return base * row_scale * col_scale


def block_scale(stream_key, shape, cuts, smallest, top_value):
    gain, own = 1.0, jax.random.fold_in(stream_key, 6)
    for axis_at, parts in cuts:
        heights = jnp.exp(jax.random.uniform(jax.random.fold_in(own, axis_at), (parts,), jnp.float32, smallest / len(cuts), top_value / len(cuts)))
        gain = gain * jnp.repeat(heights, shape[axis_at] // parts).reshape([-1 if axis == axis_at else 1 for axis in range(len(shape))])
    return gain


def scatter_about(rng, dims, width, most, pieces=(), kind=jnp.bfloat16):
    result = width * jax.random.normal(rng, dims, jnp.float32)
    if pieces:
        result = result * block_scale(rng, dims, pieces, -0.22, 0.18)
    return jnp.clip(result, -most, most).astype(kind)


def setup_inputs(seed: int = 0) -> dict:
    key_of = jax.random.split(jax.random.key(seed), 5)
    master = draw_master(jax.random.fold_in(key_of[4], 71), 0)
    grad = scatter_about(key_of[1], (ROWS, COLS), 1.0, 6.0, ((0, 32), (1, 16)), jnp.float32)
    moment = scatter_about(key_of[2], (ROWS, COLS), 0.3, 4.0, ((0, 32), (1, 16)), jnp.float32)
    second = jnp.clip(jnp.exp(math.log(2.0) - 2.9957323 * jax.random.uniform(key_of[3], (ROWS, COLS), jnp.float32) ** block_scale(key_of[3], (ROWS, COLS), ((0, 32), (1, 16)), -0.2, 0.2)), 0.1, 2.0)
    return {"master": master, "grad": grad, "moment": moment, "second": second}


beta_one = 0.9
beta_two = 0.95
learn_rate = 0.01
decay_rate = 0.1
epsilon = 1e-08
scale_eps = 1e-05
correct_one = 1.0 - 0.9 ** 10
correct_two = 1.0 - 0.95 ** 10

def reference(master, grad, moment, second):
    new_moment = beta_one * moment + (1.0 - beta_one) * grad
    new_second = beta_two * second + (1.0 - beta_two) * grad * grad
    update = new_moment / correct_one / (jnp.sqrt(new_second / correct_two) + epsilon) + decay_rate * master
    new_master = master - learn_rate * update
    blocked = new_master.reshape(ROWS // BLOCK, BLOCK, COLS // BLOCK, BLOCK)
    block_scales = lax.optimization_barrier(jnp.max(jnp.abs(blocked), axis=(1, 3))) + scale_eps
    forward_copy = (blocked / block_scales[:, None, :, None]).reshape(ROWS, COLS).astype(jnp.bfloat16)
    transposed_copy = forward_copy.reshape(ROWS, N_TENSOR, COLS // N_TENSOR).transpose(1, 2, 0)
    return (new_master, new_moment, new_second, block_scales, forward_copy, transposed_copy)
```

```python
import jax
import jax.numpy as jnp
from jax import lax
from jax.experimental import pallas as pl
from jax.experimental.pallas import tpu as pltpu
from jax.sharding import PartitionSpec as P

BLOCK = 128
beta_one = 0.9
beta_two = 0.95
learn_rate = 0.01
decay_rate = 0.1
epsilon = 1e-08
scale_eps = 1e-05
correct_one = 1.0 - 0.9**10
correct_two = 1.0 - 0.95**10


def step(master, grad, moment, second):
    new_moment = beta_one * moment + (1.0 - beta_one) * grad
    new_second = beta_two * second + (1.0 - beta_two) * grad * grad
    update = (
        new_moment / correct_one / (jnp.sqrt(new_second / correct_two) + epsilon)
        + decay_rate * master
    )
    return master - learn_rate * update, new_moment, new_second


def scaled_block(new_master):
    scale = jnp.max(jnp.abs(new_master)) + scale_eps
    return new_master / scale, scale


def flip_kernel(master_ref, grad_ref, moment_ref, second_ref, flip_ref):
    height, width = master_ref.shape
    for j in range(width // BLOCK):
        cols = slice(j * BLOCK, (j + 1) * BLOCK)
        new_master, _, _ = step(master_ref[:, cols], grad_ref[:, cols], moment_ref[:, cols], second_ref[:, cols])
        scaled, _ = scaled_block(new_master)
        flip_ref[cols, :] = scaled.T.astype(jnp.bfloat16)


def step_kernel(master_ref, grad_ref, moment_ref, second_ref, out_master, out_moment, out_second, scale_ref, copies_ref):
    height, width = master_ref.shape
    for j in range(width // BLOCK):
        cols = slice(j * BLOCK, (j + 1) * BLOCK)
        new_master, new_moment, new_second = step(
            master_ref[:, cols], grad_ref[:, cols], moment_ref[:, cols], second_ref[:, cols]
        )
        out_master[:, cols] = new_master
        out_moment[:, cols] = new_moment
        out_second[:, cols] = new_second
        scaled, scale = scaled_block(new_master)
        scale_ref[0, j] = scale
        low = scaled.astype(jnp.bfloat16)
        for k in range(copies_ref.shape[0]):
            copies_ref[k, :, cols] = low


def body(master, grad, moment, second):
    height, width = master.shape
    n_dp, n_tensor = lax.axis_size("dp"), lax.axis_size("tensor")
    half = n_tensor // 2
    f32, bf16 = jnp.float32, jnp.bfloat16
    whole = pl.BlockSpec(memory_space=pltpu.VMEM)
    flipped = pl.pallas_call(
        flip_kernel,
        out_shape=jax.ShapeDtypeStruct((width, height), bf16),
        in_specs=[whole] * 4,
        out_specs=whole,
        cost_estimate=pl.CostEstimate(flops=20 * height * width, bytes_accessed=16 * height * width, transcendentals=0),
        name="flip",
    )(master, grad, moment, second)
    same = jax.ShapeDtypeStruct((height, width), f32)
    new_master, new_moment, new_second, block_scales, copies = pl.pallas_call(
        step_kernel,
        out_shape=(same, same, same, jax.ShapeDtypeStruct((1, width // BLOCK), f32), jax.ShapeDtypeStruct((half, height, width), bf16)),
        in_specs=[whole] * 4,
        out_specs=(whole, whole, whole, pl.BlockSpec(memory_space=pltpu.SMEM), whole),
        cost_estimate=pl.CostEstimate(flops=20 * height * width, bytes_accessed=48 * height * width, transcendentals=0),
        name="step",
    )(master, grad, moment, second)
    same_core = [[2 * i + c for i in range(half)] for c in range(2)]
    swap = [(i, i ^ 1) for i in range(n_tensor)]
    pieces = lax.all_to_all(flipped.reshape(n_dp, width // n_dp, height), "dp", 0, 0, tiled=True)
    mine_f = lax.all_to_all(copies, "tensor", 0, 0, tiled=True, axis_index_groups=same_core)
    mine_t = lax.all_to_all(jnp.broadcast_to(pieces[None], (half, *pieces.shape)), "tensor", 0, 0, tiled=True, axis_index_groups=same_core)
    other_f = lax.ppermute(mine_f, "tensor", swap)
    other_t = lax.ppermute(mine_t, "tensor", swap)
    first = lax.axis_index("tensor") % 2 == 0
    both_f = jnp.where(first, jnp.stack([mine_f, other_f], 1), jnp.stack([other_f, mine_f], 1))
    forward_copy = both_f.reshape(n_tensor, height, width).transpose(1, 0, 2).reshape(height, n_tensor * width)
    both_t = jnp.where(first, jnp.stack([mine_t, other_t], 1), jnp.stack([other_t, mine_t], 1))
    transposed_copy = both_t.reshape(n_tensor, n_dp, width // n_dp, height).transpose(0, 2, 1, 3).reshape(n_tensor, width // n_dp, n_dp * height)
    return (new_master, new_moment, new_second, block_scales, forward_copy, transposed_copy)


def solution(mesh):
    spec = P("dp", "tensor")
    return jax.shard_map(
        body,
        mesh=mesh,
        in_specs=(spec,) * 4,
        out_specs=(spec, spec, spec, spec, P("dp", None), P(None, "dp", None)),
        check_vma=False,
    )
```

```python
import jax
import jax.numpy as jnp
from jax import lax
from jax.experimental import pallas as pl
from jax.experimental.pallas import tpu as pltpu
from jax.sharding import PartitionSpec as P

BLOCK = 128
beta_one = 0.9
beta_two = 0.95
learn_rate = 0.01
decay_rate = 0.1
epsilon = 1e-08
scale_eps = 1e-05
correct_one = 1.0 - 0.9**10
correct_two = 1.0 - 0.95**10


def step(master, grad, moment, second):
    new_moment = beta_one * moment + (1.0 - beta_one) * grad
    new_second = beta_two * second + (1.0 - beta_two) * grad * grad
    update = (
        new_moment / correct_one / (jnp.sqrt(new_second / correct_two) + epsilon)
        + decay_rate * master
    )
    return master - learn_rate * update, new_moment, new_second


def scaled_block(new_master):
    scale = jnp.max(jnp.abs(new_master)) + scale_eps
    return new_master / scale, scale


def visit(n, first):
    rest = [k for k in range(n) if k != first]
    return [first] + sorted(rest, key=lambda k: (-min(abs(k - first), n - abs(k - first)), k))


def flip_kernel(order, master_ref, grad_ref, moment_ref, second_ref, flip_ref, low_ref):
    height, width = master_ref.shape
    rows = width // len(order)
    for j in range(width // BLOCK):
        cols = slice(j * BLOCK, (j + 1) * BLOCK)
        new_master, _, _ = step(master_ref[:, cols], grad_ref[:, cols], moment_ref[:, cols], second_ref[:, cols])
        scaled, _ = scaled_block(new_master)
        flipped = scaled.T.astype(jnp.bfloat16)
        for k, owner in enumerate(order):
            if owner * rows // BLOCK == j:
                at = owner * rows - j * BLOCK
                flip_ref[k * rows : (k + 1) * rows, :] = flipped[at : at + rows]
        low_ref[j * height : (j + 1) * height, :] = scaled.astype(jnp.bfloat16)


def step_kernel(master_ref, grad_ref, moment_ref, second_ref, low_ref, out_master, out_moment, out_second, scale_ref, both_ref, sem):
    rows = low_ref.shape[0]
    copies = [pltpu.make_async_copy(low_ref, both_ref.at[k, :rows], sem) for k in range(both_ref.shape[0])]
    for copy in copies:
        copy.start()
    height, width = master_ref.shape
    for j in range(width // BLOCK):
        cols = slice(j * BLOCK, (j + 1) * BLOCK)
        new_master, new_moment, new_second = step(
            master_ref[:, cols], grad_ref[:, cols], moment_ref[:, cols], second_ref[:, cols]
        )
        out_master[:, cols] = new_master
        out_moment[:, cols] = new_moment
        out_second[:, cols] = new_second
        _, scale = scaled_block(new_master)
        scale_ref[0, j] = scale
    for copy in copies:
        copy.wait()


def pack_kernel(order, pieces_ref, _, both_ref, slab, sem):
    rows = pieces_ref.shape[0]
    part = rows // len(order)
    for k, owner in enumerate(order):
        slab[owner * part : (owner + 1) * part, :] = pieces_ref[k * part : (k + 1) * part, :]
    copies = [pltpu.make_async_copy(slab, both_ref.at[k, rows:], sem) for k in range(both_ref.shape[0])]
    for copy in copies:
        copy.start()
    for copy in copies:
        copy.wait()


def place_kernel(order, flip, both_ref, *refs):
    forward_ref, flipped_ref, sem = refs[-3:]
    chips, rows2, _ = both_ref.shape
    rows = rows2 // 2
    height = forward_ref.shape[0]
    width = rows * BLOCK // height
    core = (lax.axis_index("tensor") & 1) ^ flip
    copies = []
    for k, chip in enumerate(order):
        slab = 2 * chip + core
        copies.append(pltpu.make_async_copy(both_ref.at[k, rows:, :], flipped_ref.at[slab], sem))
        for j in range(width // BLOCK):
            start = pl.multiple_of(slab * width + j * BLOCK, BLOCK)
            copies.append(
                pltpu.make_async_copy(
                    both_ref.at[k, j * height : (j + 1) * height, :], forward_ref.at[:, pl.ds(start, BLOCK)], sem
                )
            )
    for copy in copies:
        copy.start()
    for copy in copies:
        copy.wait()


def in_vmem(x):
    return pltpu.with_memory_space_constraint(x, pltpu.VMEM)


whole = pl.BlockSpec(memory_space=pltpu.VMEM)
hbm = pl.BlockSpec(memory_space=pl.ANY)


def place(order, flip, both, height, n_tensor, outs):
    rows = both.shape[1] // 2
    width = rows * BLOCK // height
    return pl.pallas_call(
        lambda *refs: place_kernel(order, flip, *refs),
        out_shape=(
            jax.ShapeDtypeStruct((height, n_tensor * width), jnp.bfloat16),
            jax.ShapeDtypeStruct((n_tensor, rows, BLOCK), jnp.bfloat16),
        ),
        in_specs=[whole] + [hbm] * len(outs),
        out_specs=(hbm, hbm),
        scratch_shapes=[pltpu.SemaphoreType.DMA],
        input_output_aliases={1 + i: i for i in range(len(outs))},
        cost_estimate=pl.CostEstimate(flops=0, bytes_accessed=4 * both.size, transcendentals=0),
        name="place_other" if flip else "place_mine",
    )(in_vmem(both), *outs)


def body(master, grad, moment, second):
    height, width = master.shape
    n_dp, n_tensor = lax.axis_size("dp"), lax.axis_size("tensor")
    half = n_tensor // 2
    f32, bf16 = jnp.float32, jnp.bfloat16
    rows = height * width // BLOCK
    z_order = visit(n_dp // 2, n_dp // 4)
    chip_order = visit(half, half // 2 + 1)
    flipped, low = pl.pallas_call(
        lambda *refs: flip_kernel(z_order, *refs),
        out_shape=(jax.ShapeDtypeStruct((width, height), bf16), jax.ShapeDtypeStruct((rows, BLOCK), bf16)),
        in_specs=[whole] * 4,
        out_specs=(whole, whole),
        cost_estimate=pl.CostEstimate(flops=20 * height * width, bytes_accessed=16 * height * width, transcendentals=0),
        name="flip",
    )(master, grad, moment, second)
    same = jax.ShapeDtypeStruct((height, width), f32)
    new_master, new_moment, new_second, block_scales, both = pl.pallas_call(
        step_kernel,
        out_shape=(same, same, same, jax.ShapeDtypeStruct((1, width // BLOCK), f32), jax.ShapeDtypeStruct((half, 2 * rows, BLOCK), bf16)),
        in_specs=[whole] * 5,
        out_specs=(whole, whole, whole, pl.BlockSpec(memory_space=pltpu.SMEM), hbm),
        scratch_shapes=[pltpu.SemaphoreType.DMA],
        cost_estimate=pl.CostEstimate(flops=20 * height * width, bytes_accessed=30 * height * width, transcendentals=0),
        name="step",
    )(master, grad, moment, second, low)
    dp_order = [[2 * z + y for z in z_order for y in range(2)]]
    pieces = lax.all_to_all(flipped.reshape(n_dp, width // n_dp, height), "dp", 0, 0, tiled=True, axis_index_groups=dp_order)
    both = pl.pallas_call(
        lambda *refs: pack_kernel(z_order, *refs),
        out_shape=jax.ShapeDtypeStruct(both.shape, bf16),
        in_specs=[whole, hbm],
        out_specs=hbm,
        scratch_shapes=[pltpu.VMEM((rows, BLOCK), bf16), pltpu.SemaphoreType.DMA],
        input_output_aliases={1: 0},
        name="pack",
    )(in_vmem(pieces.reshape(rows, BLOCK)), both)
    same_core = [[2 * k + c for k in chip_order] for c in range(2)]
    mine = lax.all_to_all(both, "tensor", 0, 0, tiled=True, axis_index_groups=same_core)
    other = lax.ppermute(mine, "tensor", [(i, i ^ 1) for i in range(n_tensor)])
    outs = place(chip_order, 0, mine, height, n_tensor, ())
    forward_copy, slabs = place(chip_order, 1, other, height, n_tensor, outs)
    transposed_copy = slabs.reshape(n_tensor, n_dp, width // n_dp, height).transpose(0, 2, 1, 3).reshape(n_tensor, width // n_dp, n_dp * height)
    return (new_master, new_moment, new_second, block_scales, forward_copy, transposed_copy)


def solution(mesh):
    spec = P("dp", "tensor")
    return jax.shard_map(
        body,
        mesh=mesh,
        in_specs=(spec,) * 4,
        out_specs=(spec, spec, spec, spec, P("dp", None), P(None, "dp", None)),
        check_vma=False,
    )
```

```python
import jax
import jax.numpy as jnp
from jax import lax
from jax.experimental import pallas as pl
from jax.experimental.pallas import tpu as pltpu
from jax.sharding import PartitionSpec as P

BLOCK = 128
beta_one = 0.9
beta_two = 0.95
learn_rate = 0.01
decay_rate = 0.1
epsilon = 1e-08
scale_eps = 1e-05
correct_one = 1.0 - 0.9**10
correct_two = 1.0 - 0.95**10


def step(master, grad, moment, second):
    new_moment = beta_one * moment + (1.0 - beta_one) * grad
    new_second = beta_two * second + (1.0 - beta_two) * grad * grad
    update = (
        new_moment / correct_one / (jnp.sqrt(new_second / correct_two) + epsilon)
        + decay_rate * master
    )
    return master - learn_rate * update, new_moment, new_second


def scaled_block(new_master):
    scale = jnp.max(jnp.abs(new_master)) + scale_eps
    return new_master / scale, scale


def visit(n, first):
    rest = [k for k in range(n) if k != first]
    return [first] + sorted(rest, key=lambda k: (-min(abs(k - first), n - abs(k - first)), k))


def flip_kernel(order, master_ref, grad_ref, moment_ref, second_ref, own_ref):
    height, width = master_ref.shape
    rows = width // len(order)
    for j in range(width // BLOCK):
        cols = slice(j * BLOCK, (j + 1) * BLOCK)
        new_master, _, _ = step(master_ref[:, cols], grad_ref[:, cols], moment_ref[:, cols], second_ref[:, cols])
        scaled, _ = scaled_block(new_master)
        flipped = scaled.T.astype(jnp.bfloat16)
        for k, owner in enumerate(order):
            if owner * rows // BLOCK == j:
                at = owner * rows - j * BLOCK
                own_ref[k * rows : (k + 1) * rows, :] = flipped[at : at + rows]
        own_ref[width + j * height : width + (j + 1) * height, :] = scaled.astype(jnp.bfloat16)


def repeat_kernel(load_ref, copies_ref):
    for k in range(copies_ref.shape[0]):
        copies_ref[k] = load_ref[...]


def spread_kernel(order, load_ref, copies_ref):
    sides, slabs = load_ref.shape[:2]
    for side in range(sides):
        for s in range(slabs):
            for k, owner in enumerate(order):
                tile = load_ref[side, s, k]
                for n in range(copies_ref.shape[0]):
                    copies_ref[n, side, s, owner] = tile


def place_own(forward_order, flipped_order, flip, slabs_ref, forward_ref, flipped_ref, sem, work=None):
    core = (lax.axis_index("tensor") & 1) ^ flip
    width = forward_ref.shape[2] // slabs_ref.shape[0]

    def forward():
        copies = []
        for k, chip in enumerate(forward_order):
            for s in range(2):
                for j in range(width // BLOCK):
                    start = (2 * chip + s) * width + j * BLOCK
                    copies.append(
                        pltpu.make_async_copy(
                            slabs_ref.at[2 * k + s, j], forward_ref.at[:, :, start : start + BLOCK], sem
                        )
                    )
        return copies

    def flipped():
        copies = []
        for p, (chip, side) in enumerate(flipped_order):
            for s in range(2):
                copies.append(pltpu.make_async_copy(slabs_ref.at[p, s], flipped_ref.at[2 * chip + s, :, side], sem))
        return copies

    for which, copies in ((0, forward), (1, flipped)):

        @pl.when(core == which)
        def _(copies=copies):
            for copy in copies():
                copy.start()

    if work is not None:
        work()

    for which, copies in ((0, forward), (1, flipped)):

        @pl.when(core == which)
        def _(copies=copies):
            for copy in copies():
                copy.wait()


def finish_kernel(orders, slabs_ref, master_ref, grad_ref, moment_ref, second_ref, forward_ref, flipped_ref, out_master, out_moment, out_second, scale_ref, sem):
    def work():
        height, width = master_ref.shape
        for j in range(width // BLOCK):
            cols = slice(j * BLOCK, (j + 1) * BLOCK)
            new_master, new_moment, new_second = step(
                master_ref[:, cols], grad_ref[:, cols], moment_ref[:, cols], second_ref[:, cols]
            )
            out_master[:, cols] = new_master
            out_moment[:, cols] = new_moment
            out_second[:, cols] = new_second
            _, scale = scaled_block(new_master)
            scale_ref[0, j] = scale

    place_own(*orders, 0, slabs_ref, forward_ref, flipped_ref, sem, work)


def place_kernel(orders, slabs_ref, _, __, forward_ref, flipped_ref, sem):
    place_own(*orders, 1, slabs_ref, forward_ref, flipped_ref, sem)


def in_vmem(x):
    return pltpu.with_memory_space_constraint(x, pltpu.VMEM)


whole = pl.BlockSpec(memory_space=pltpu.VMEM)
hbm = pl.BlockSpec(memory_space=pl.ANY)


def body(master, grad, moment, second):
    height, width = master.shape
    n_dp, n_tensor = lax.axis_size("dp"), lax.axis_size("tensor")
    n_z, n_chip, n_side, tile = n_dp // 2, n_tensor // 2, 2, 8
    f32, bf16 = jnp.float32, jnp.bfloat16
    rows = height * width // BLOCK
    z_order = visit(n_z, n_z // 2)
    chip_order = visit(n_chip, n_chip // 2 + 1)
    plane_order = [(chip, side) for chip in chip_order for side in range(n_side)]
    orders = (chip_order, plane_order)
    own = pl.pallas_call(
        lambda *refs: flip_kernel(z_order, *refs),
        out_shape=pltpu.VMEM((2 * rows, BLOCK), bf16),
        in_specs=[whole] * 4,
        out_specs=whole,
        cost_estimate=pl.CostEstimate(flops=20 * height * width, bytes_accessed=16 * height * width, transcendentals=0),
        name="flip",
    )(master, grad, moment, second)
    both = lax.all_gather(own, "tensor", axis=0, axis_index_groups=[[2 * k, 2 * k + 1] for k in range(n_chip)])

    def forward_part(both):
        copies = pl.pallas_call(
            repeat_kernel,
            out_shape=pltpu.VMEM((n_chip, 2 * rows, BLOCK), bf16),
            in_specs=[whole],
            out_specs=whole,
            name="repeat",
        )(in_vmem(both[:, rows:].reshape(2 * rows, BLOCK)))
        groups = [[2 * k + c for k in chip_order] for c in range(2)]
        slabs = lax.all_to_all(copies, "tensor", 0, 0, tiled=True, axis_index_groups=groups)
        return slabs.reshape(n_tensor, width // BLOCK, height // tile, tile, BLOCK)

    def flipped_part(both):
        pieces = both[:, :rows].reshape(2, n_z, n_side, tile, BLOCK).transpose(1, 2, 0, 3, 4)
        groups = [[n_side * z + side for z in z_order] for side in range(n_side)]
        pieces = lax.all_to_all(pieces, "dp", 0, 0, tiled=True, axis_index_groups=groups)
        copies = pl.pallas_call(
            lambda *refs: spread_kernel(z_order, *refs),
            out_shape=pltpu.VMEM((n_chip, n_side, 2, n_z, tile, BLOCK), bf16),
            in_specs=[whole],
            out_specs=whole,
            name="spread",
        )(in_vmem(pieces.transpose(1, 2, 0, 3, 4)))
        groups = [
            [(n_side * z + side) * n_tensor + 2 * chip + c for chip, side in plane_order] for z in range(n_z) for c in range(2)
        ]
        slabs = lax.all_to_all(
            copies.reshape(n_chip * n_side, 2, n_z, tile, BLOCK), ("dp", "tensor"), 0, 0, tiled=True, axis_index_groups=groups
        )
        return slabs.reshape(n_tensor, width // BLOCK, height // tile, tile, BLOCK)

    mine = lax.cond(lax.axis_index("tensor") % 2 == 1, flipped_part, forward_part, both)
    other = lax.ppermute(mine, "tensor", [(i, i ^ 1) for i in range(n_tensor)])
    same = jax.ShapeDtypeStruct((height, width), f32)
    outs = (
        jax.ShapeDtypeStruct((height // tile, tile, n_tensor * width), bf16),
        jax.ShapeDtypeStruct((n_tensor, n_z, n_side, tile, BLOCK), bf16),
    )
    forward_copy, transposed_copy, new_master, new_moment, new_second, block_scales = pl.pallas_call(
        lambda *refs: finish_kernel(orders, *refs),
        out_shape=(*outs, same, same, same, jax.ShapeDtypeStruct((1, width // BLOCK), f32)),
        in_specs=[whole] * 5,
        out_specs=(hbm, hbm, whole, whole, whole, pl.BlockSpec(memory_space=pltpu.SMEM)),
        scratch_shapes=[pltpu.SemaphoreType.DMA],
        cost_estimate=pl.CostEstimate(flops=20 * height * width, bytes_accessed=4 * mine.size, transcendentals=0),
        name="finish",
    )(in_vmem(mine), *(in_vmem(x) for x in (master, grad, moment, second)))
    forward_copy, transposed_copy = pl.pallas_call(
        lambda *refs: place_kernel(orders, *refs),
        out_shape=outs,
        in_specs=[whole, hbm, hbm],
        out_specs=(hbm, hbm),
        scratch_shapes=[pltpu.SemaphoreType.DMA],
        input_output_aliases={1: 0, 2: 1},
        cost_estimate=pl.CostEstimate(flops=0, bytes_accessed=4 * mine.size, transcendentals=0),
        name="place",
    )(in_vmem(other), forward_copy, transposed_copy)
    forward_copy = forward_copy.reshape(height, n_tensor * width)
    transposed_copy = transposed_copy.reshape(n_tensor, n_dp, tile, BLOCK).transpose(0, 2, 1, 3).reshape(n_tensor, tile, n_dp * BLOCK)
    return (new_master, new_moment, new_second, block_scales, forward_copy, transposed_copy)


def solution(mesh):
    spec = P("dp", "tensor")
    return jax.shard_map(
        body,
        mesh=mesh,
        in_specs=(spec,) * 4,
        out_specs=(spec, spec, spec, spec, P("dp", None), P(None, "dp", None)),
        check_vma=False,
    )
```

```python
import jax
import jax.numpy as jnp
from jax import lax
from jax.experimental import pallas as pl
from jax.experimental.pallas import tpu as pltpu
from jax.sharding import PartitionSpec as P

BLOCK = 128
beta_one = 0.9
beta_two = 0.95
learn_rate = 0.01
decay_rate = 0.1
epsilon = 1e-08
scale_eps = 1e-05
correct_one = 1.0 - 0.9**10
correct_two = 1.0 - 0.95**10


def step(master, grad, moment, second):
    new_moment = beta_one * moment + (1.0 - beta_one) * grad
    new_second = beta_two * second + (1.0 - beta_two) * grad * grad
    update = (
        new_moment / correct_one / (jnp.sqrt(new_second / correct_two) + epsilon)
        + decay_rate * master
    )
    return master - learn_rate * update, new_moment, new_second


def scaled_block(new_master):
    scale = jnp.max(jnp.abs(new_master)) + scale_eps
    return new_master / scale, scale


def z_visit(n):
    lead = n // 2 + 1
    far = [k for k in (0, 8, 1, 10, 2, 7, 15, 11, 3, 6, 14, 12, 4, 5, 13) if k < n and k != lead]
    rest = [k for k in range(n) if k != lead and k not in far]
    return [lead] + far + rest


def plane_visit(nx, ny, n_side):
    pairs = [((nx // 2 - i) % nx, (ny // 2 - j) % ny) for j in range(ny) for i in range(nx)]
    return [(x * (ny // n_side) + y // n_side, y % n_side) for x, y in pairs]


def flip_kernel(order, master_ref, grad_ref, moment_ref, second_ref, own_ref):
    height, width = master_ref.shape
    rows = width // len(order)
    for j in range(width // BLOCK):
        cols = slice(j * BLOCK, (j + 1) * BLOCK)
        new_master, _, _ = step(master_ref[:, cols], grad_ref[:, cols], moment_ref[:, cols], second_ref[:, cols])
        scaled, _ = scaled_block(new_master)
        flipped = scaled.T.astype(jnp.bfloat16)
        for k, owner in enumerate(order):
            if owner * rows // BLOCK == j:
                at = owner * rows - j * BLOCK
                own_ref[k * rows : (k + 1) * rows, :] = flipped[at : at + rows]
        own_ref[width + j * height : width + (j + 1) * height, :] = scaled.astype(jnp.bfloat16)


def repeat_kernel(load_ref, copies_ref):
    for k in range(copies_ref.shape[0]):
        copies_ref[k] = load_ref[...]


def spread_kernel(z_order, plane_order, load_ref, copies_ref):
    sides, slabs = load_ref.shape[:2]
    for side in range(sides):
        for s in range(slabs):
            for k, owner in enumerate(z_order):
                tile = load_ref[side, s, k]
                for n, (_, its) in enumerate(plane_order):
                    if its == side:
                        copies_ref[n, s, owner] = tile


def place_own(forward_order, flipped_order, flip, slabs_ref, forward_ref, flipped_ref, sem, work=None):
    core = (lax.axis_index("tensor") & 1) ^ flip
    width = forward_ref.shape[2] // slabs_ref.shape[0]

    def forward():
        copies = []
        for k, chip in enumerate(forward_order):
            for s in range(2):
                for j in range(width // BLOCK):
                    start = (2 * chip + s) * width + j * BLOCK
                    copies.append(
                        pltpu.make_async_copy(
                            slabs_ref.at[2 * k + s, j], forward_ref.at[:, :, start : start + BLOCK], sem
                        )
                    )
        return copies

    def flipped():
        copies = []
        for p, (chip, side) in enumerate(flipped_order):
            for s in range(2):
                copies.append(pltpu.make_async_copy(slabs_ref.at[p, s], flipped_ref.at[2 * chip + s, :, side], sem))
        return copies

    for which, copies in ((0, forward), (1, flipped)):

        @pl.when(core == which)
        def _(copies=copies):
            for n, copy in enumerate(copies()):
                copy.start(priority=n % 2)

    if work is not None:
        work()

    for which, copies in ((0, forward), (1, flipped)):

        @pl.when(core == which)
        def _(copies=copies):
            for copy in copies():
                copy.wait()


def finish_kernel(orders, slabs_ref, master_ref, grad_ref, moment_ref, second_ref, forward_ref, flipped_ref, out_master, out_moment, out_second, scale_ref, sem):
    def work():
        height, width = master_ref.shape
        for j in range(width // BLOCK):
            cols = slice(j * BLOCK, (j + 1) * BLOCK)
            new_master, new_moment, new_second = step(
                master_ref[:, cols], grad_ref[:, cols], moment_ref[:, cols], second_ref[:, cols]
            )
            out_master[:, cols] = new_master
            out_moment[:, cols] = new_moment
            out_second[:, cols] = new_second
            _, scale = scaled_block(new_master)
            scale_ref[0, j] = scale

    place_own(*orders, 0, slabs_ref, forward_ref, flipped_ref, sem, work)


def place_kernel(orders, slabs_ref, _, __, forward_ref, flipped_ref, sem):
    place_own(*orders, 1, slabs_ref, forward_ref, flipped_ref, sem)


def in_vmem(x):
    return pltpu.with_memory_space_constraint(x, pltpu.VMEM)


whole = pl.BlockSpec(memory_space=pltpu.VMEM)
hbm = pl.BlockSpec(memory_space=pl.ANY)


def body(master, grad, moment, second):
    height, width = master.shape
    n_dp, n_tensor = lax.axis_size("dp"), lax.axis_size("tensor")
    n_z, n_chip, n_side, tile = n_dp // 2, n_tensor // 2, 2, 8
    f32, bf16 = jnp.float32, jnp.bfloat16
    rows = height * width // BLOCK
    z_order = z_visit(n_z)
    chip_order = [(n_chip // 2 + 1 + k) % n_chip for k in range(n_chip)]
    plane_order = plane_visit(4, n_chip // 4 * n_side, n_side)
    orders = (chip_order, plane_order)
    own = pl.pallas_call(
        lambda *refs: flip_kernel(z_order, *refs),
        out_shape=pltpu.VMEM((2 * rows, BLOCK), bf16),
        in_specs=[whole] * 4,
        out_specs=whole,
        cost_estimate=pl.CostEstimate(flops=20 * height * width, bytes_accessed=16 * height * width, transcendentals=0),
        name="flip",
    )(master, grad, moment, second)
    both = lax.all_gather(own, "tensor", axis=0, axis_index_groups=[[2 * k, 2 * k + 1] for k in range(n_chip)])

    def forward_part(both):
        copies = pl.pallas_call(
            repeat_kernel,
            out_shape=pltpu.VMEM((n_chip, 2 * rows, BLOCK), bf16),
            in_specs=[whole],
            out_specs=whole,
            name="repeat",
        )(in_vmem(both[:, rows:].reshape(2 * rows, BLOCK)))
        groups = [[2 * k + c for k in chip_order] for c in range(2)]
        slabs = lax.all_to_all(copies, "tensor", 0, 0, tiled=True, axis_index_groups=groups)
        return slabs.reshape(n_tensor, width // BLOCK, height // tile, tile, BLOCK)

    def flipped_part(both):
        pieces = both[:, :rows].reshape(2, n_z, n_side, tile, BLOCK).transpose(1, 2, 0, 3, 4)
        groups = [[n_side * z + side for z in z_order] for side in range(n_side)]
        pieces = lax.all_to_all(pieces, "dp", 0, 0, tiled=True, axis_index_groups=groups)
        copies = pl.pallas_call(
            lambda *refs: spread_kernel(z_order, plane_order, *refs),
            out_shape=pltpu.VMEM((n_tensor, 2, n_z, tile, BLOCK), bf16),
            in_specs=[whole],
            out_specs=whole,
            name="spread",
        )(in_vmem(pieces.transpose(1, 2, 0, 3, 4)))
        groups = [
            [(n_side * z + side) * n_tensor + 2 * chip + c for chip, side in plane_order] for z in range(n_z) for c in range(2)
        ]
        slabs = lax.all_to_all(
            copies, ("dp", "tensor"), 0, 0, tiled=True, axis_index_groups=groups
        )
        return slabs.reshape(n_tensor, width // BLOCK, height // tile, tile, BLOCK)

    mine = lax.cond(lax.axis_index("tensor") % 2 == 1, flipped_part, forward_part, both)
    other = lax.ppermute(mine, "tensor", [(i, i ^ 1) for i in range(n_tensor)])
    same = jax.ShapeDtypeStruct((height, width), f32)
    outs = (
        jax.ShapeDtypeStruct((height // tile, tile, n_tensor * width), bf16),
        jax.ShapeDtypeStruct((n_tensor, n_z, n_side, tile, BLOCK), bf16),
    )
    forward_copy, transposed_copy, new_master, new_moment, new_second, block_scales = pl.pallas_call(
        lambda *refs: finish_kernel(orders, *refs),
        out_shape=(*outs, same, same, same, jax.ShapeDtypeStruct((1, width // BLOCK), f32)),
        in_specs=[whole] * 5,
        out_specs=(hbm, hbm, whole, whole, whole, pl.BlockSpec(memory_space=pltpu.SMEM)),
        scratch_shapes=[pltpu.SemaphoreType.DMA],
        cost_estimate=pl.CostEstimate(flops=20 * height * width, bytes_accessed=4 * mine.size, transcendentals=0),
        name="finish",
    )(in_vmem(mine), *(in_vmem(x) for x in (master, grad, moment, second)))
    forward_copy, transposed_copy = pl.pallas_call(
        lambda *refs: place_kernel(orders, *refs),
        out_shape=outs,
        in_specs=[whole, hbm, hbm],
        out_specs=(hbm, hbm),
        scratch_shapes=[pltpu.SemaphoreType.DMA],
        input_output_aliases={1: 0, 2: 1},
        cost_estimate=pl.CostEstimate(flops=0, bytes_accessed=4 * mine.size, transcendentals=0),
        name="place",
    )(in_vmem(other), forward_copy, transposed_copy)
    forward_copy = forward_copy.reshape(height, n_tensor * width)
    transposed_copy = transposed_copy.reshape(n_tensor, n_dp, tile, BLOCK).transpose(0, 2, 1, 3).reshape(n_tensor, tile, n_dp * BLOCK)
    return (new_master, new_moment, new_second, block_scales, forward_copy, transposed_copy)


def solution(mesh):
    spec = P("dp", "tensor")
    return jax.shard_map(
        body,
        mesh=mesh,
        in_specs=(spec,) * 4,
        out_specs=(spec, spec, spec, spec, P("dp", None), P(None, "dp", None)),
        check_vma=False,
    )
```

```python
import jax
import jax.numpy as jnp
from jax import lax
from jax.experimental import pallas as pl
from jax.experimental.pallas import tpu as pltpu
from jax.sharding import PartitionSpec as P

BLOCK = 128
beta_one = 0.9
beta_two = 0.95
learn_rate = 0.01
decay_rate = 0.1
epsilon = 1e-08
scale_eps = 1e-05
correct_one = 1.0 - 0.9**10
correct_two = 1.0 - 0.95**10


def step(master, grad, moment, second):
    new_moment = beta_one * moment + (1.0 - beta_one) * grad
    new_second = beta_two * second + (1.0 - beta_two) * grad * grad
    update = (
        new_moment / correct_one / (jnp.sqrt(new_second / correct_two) + epsilon)
        + decay_rate * master
    )
    return master - learn_rate * update, new_moment, new_second


def scaled_block(new_master):
    scale = jnp.max(jnp.abs(new_master)) + scale_eps
    return new_master / scale, scale


def z_visit(n):
    lead = n // 2 + 1
    far = [k for k in (0, 8, 1, 10, 2, 7, 15, 11, 3, 6, 14, 12, 4, 5, 13) if k < n and k != lead]
    rest = [k for k in range(n) if k != lead and k not in far]
    return [lead] + far + rest


def plane_visit(nx, ny, n_side):
    pairs = [((nx // 2 - i) % nx, (ny // 2 - j) % ny) for j in range(ny) for i in range(nx)]
    return [(x * (ny // n_side) + y // n_side, y % n_side) for x, y in pairs]


def flip_kernel(order, master_hbm, grad_hbm, moment_hbm, second_hbm, own_ref, held, sem):
    part = master_hbm.shape[0] // 4
    copies = [
        pltpu.make_async_copy(ref.at[pl.ds(k * part, part)], held.at[n, pl.ds(k * part, part)], sem)
        for k in range(4)
        for n, ref in enumerate((master_hbm, grad_hbm, moment_hbm, second_hbm))
    ]
    for n, copy in enumerate(copies):
        copy.start(priority=n % 2)
    for copy in copies:
        copy.wait()
    master_ref, grad_ref, moment_ref, second_ref = (held.at[n] for n in range(4))
    height, width = master_hbm.shape
    rows = width // len(order)
    for j in range(width // BLOCK):
        cols = slice(j * BLOCK, (j + 1) * BLOCK)
        new_master, _, _ = step(master_ref[:, cols], grad_ref[:, cols], moment_ref[:, cols], second_ref[:, cols])
        scaled, _ = scaled_block(new_master)
        flipped = scaled.T.astype(jnp.bfloat16)
        for k, owner in enumerate(order):
            if owner * rows // BLOCK == j:
                at = owner * rows - j * BLOCK
                own_ref[k * rows : (k + 1) * rows, :] = flipped[at : at + rows]
        own_ref[width + j * height : width + (j + 1) * height, :] = scaled.astype(jnp.bfloat16)


def repeat_kernel(load_ref, copies_ref):
    for k in range(copies_ref.shape[0]):
        copies_ref[k] = load_ref[...]


def spread_kernel(z_order, plane_order, load_ref, copies_ref):
    sides, slabs = load_ref.shape[:2]
    for side in range(sides):
        for s in range(slabs):
            for k, owner in enumerate(z_order):
                tile = load_ref[side, s, k]
                for n, (_, its) in enumerate(plane_order):
                    if its == side:
                        copies_ref[n, s, owner] = tile


def place_own(forward_order, flipped_order, flip, slabs_ref, forward_ref, flipped_ref, sem, work=None):
    core = (lax.axis_index("tensor") & 1) ^ flip
    width = forward_ref.shape[2] // slabs_ref.shape[0]

    def forward():
        copies = []
        for k, chip in enumerate(forward_order):
            for s in range(2):
                for j in range(width // BLOCK):
                    start = (2 * chip + s) * width + j * BLOCK
                    copies.append(
                        pltpu.make_async_copy(
                            slabs_ref.at[2 * k + s, j], forward_ref.at[:, :, start : start + BLOCK], sem
                        )
                    )
        return copies

    def flipped():
        copies = []
        for p, (chip, side) in enumerate(flipped_order):
            for s in range(2):
                copies.append(pltpu.make_async_copy(slabs_ref.at[p, s], flipped_ref.at[2 * chip + s, :, side], sem))
        return copies

    for which, copies in ((0, forward), (1, flipped)):

        @pl.when(core == which)
        def _(copies=copies):
            for n, copy in enumerate(copies()):
                copy.start(priority=n % 2)

    if work is not None:
        work()

    for which, copies in ((0, forward), (1, flipped)):

        @pl.when(core == which)
        def _(copies=copies):
            for copy in copies():
                copy.wait()


def finish_kernel(orders, slabs_ref, master_ref, grad_ref, moment_ref, second_ref, forward_ref, flipped_ref, out_master, out_moment, out_second, scale_ref, sem):
    def work():
        height, width = master_ref.shape
        for j in range(width // BLOCK):
            cols = slice(j * BLOCK, (j + 1) * BLOCK)
            new_master, new_moment, new_second = step(
                master_ref[:, cols], grad_ref[:, cols], moment_ref[:, cols], second_ref[:, cols]
            )
            out_master[:, cols] = new_master
            out_moment[:, cols] = new_moment
            out_second[:, cols] = new_second
            _, scale = scaled_block(new_master)
            scale_ref[0, j] = scale

    place_own(*orders, 0, slabs_ref, forward_ref, flipped_ref, sem, work)


def place_kernel(orders, slabs_ref, _, __, forward_ref, flipped_ref, sem):
    place_own(*orders, 1, slabs_ref, forward_ref, flipped_ref, sem)


def in_vmem(x):
    return pltpu.with_memory_space_constraint(x, pltpu.VMEM)


whole = pl.BlockSpec(memory_space=pltpu.VMEM)
hbm = pl.BlockSpec(memory_space=pl.ANY)


def body(master, grad, moment, second):
    height, width = master.shape
    n_dp, n_tensor = lax.axis_size("dp"), lax.axis_size("tensor")
    n_z, n_chip, n_side, tile = n_dp // 2, n_tensor // 2, 2, 8
    f32, bf16 = jnp.float32, jnp.bfloat16
    rows = height * width // BLOCK
    z_order = z_visit(n_z)
    chip_order = [(n_chip // 2 + 1 + k) % n_chip for k in range(n_chip)]
    plane_order = plane_visit(4, n_chip // 4 * n_side, n_side)
    orders = (chip_order, plane_order)
    own = pl.pallas_call(
        lambda *refs: flip_kernel(z_order, *refs),
        out_shape=pltpu.VMEM((2 * rows, BLOCK), bf16),
        in_specs=[hbm] * 4,
        out_specs=whole,
        scratch_shapes=[pltpu.VMEM((4, height, width), f32), pltpu.SemaphoreType.DMA],
        cost_estimate=pl.CostEstimate(flops=20 * height * width, bytes_accessed=16 * height * width, transcendentals=0),
        name="flip",
    )(master, grad, moment, second)
    both = lax.all_gather(own, "tensor", axis=0, axis_index_groups=[[2 * k, 2 * k + 1] for k in range(n_chip)])

    def forward_part(both):
        copies = pl.pallas_call(
            repeat_kernel,
            out_shape=pltpu.VMEM((n_chip, 2 * rows, BLOCK), bf16),
            in_specs=[whole],
            out_specs=whole,
            name="repeat",
        )(in_vmem(both[:, rows:].reshape(2 * rows, BLOCK)))
        groups = [[2 * k + c for k in chip_order] for c in range(2)]
        slabs = lax.all_to_all(copies, "tensor", 0, 0, tiled=True, axis_index_groups=groups)
        return slabs.reshape(n_tensor, width // BLOCK, height // tile, tile, BLOCK)

    def flipped_part(both):
        pieces = both[:, :rows].reshape(2, n_z, n_side, tile, BLOCK).transpose(1, 2, 0, 3, 4)
        groups = [[n_side * z + side for z in z_order] for side in range(n_side)]
        pieces = lax.all_to_all(pieces, "dp", 0, 0, tiled=True, axis_index_groups=groups)
        copies = pl.pallas_call(
            lambda *refs: spread_kernel(z_order, plane_order, *refs),
            out_shape=pltpu.VMEM((n_tensor, 2, n_z, tile, BLOCK), bf16),
            in_specs=[whole],
            out_specs=whole,
            name="spread",
        )(in_vmem(pieces.transpose(1, 2, 0, 3, 4)))
        groups = [
            [(n_side * z + side) * n_tensor + 2 * chip + c for chip, side in plane_order] for z in range(n_z) for c in range(2)
        ]
        slabs = lax.all_to_all(
            copies, ("dp", "tensor"), 0, 0, tiled=True, axis_index_groups=groups
        )
        return slabs.reshape(n_tensor, width // BLOCK, height // tile, tile, BLOCK)

    mine = lax.cond(lax.axis_index("tensor") % 2 == 1, flipped_part, forward_part, both)
    other = lax.ppermute(mine, "tensor", [(i, i ^ 1) for i in range(n_tensor)])
    same = jax.ShapeDtypeStruct((height, width), f32)
    outs = (
        jax.ShapeDtypeStruct((height // tile, tile, n_tensor * width), bf16),
        jax.ShapeDtypeStruct((n_tensor, n_z, n_side, tile, BLOCK), bf16),
    )
    forward_copy, transposed_copy, new_master, new_moment, new_second, block_scales = pl.pallas_call(
        lambda *refs: finish_kernel(orders, *refs),
        out_shape=(*outs, same, same, same, jax.ShapeDtypeStruct((1, width // BLOCK), f32)),
        in_specs=[whole] * 5,
        out_specs=(hbm, hbm, whole, whole, whole, pl.BlockSpec(memory_space=pltpu.SMEM)),
        scratch_shapes=[pltpu.SemaphoreType.DMA],
        cost_estimate=pl.CostEstimate(flops=20 * height * width, bytes_accessed=4 * mine.size, transcendentals=0),
        name="finish",
    )(in_vmem(mine), *(in_vmem(x) for x in (master, grad, moment, second)))
    forward_copy, transposed_copy = pl.pallas_call(
        lambda *refs: place_kernel(orders, *refs),
        out_shape=outs,
        in_specs=[whole, hbm, hbm],
        out_specs=(hbm, hbm),
        scratch_shapes=[pltpu.SemaphoreType.DMA],
        input_output_aliases={1: 0, 2: 1},
        cost_estimate=pl.CostEstimate(flops=0, bytes_accessed=4 * mine.size, transcendentals=0),
        name="place",
    )(in_vmem(other), forward_copy, transposed_copy)
    forward_copy = forward_copy.reshape(height, n_tensor * width)
    transposed_copy = transposed_copy.reshape(n_tensor, n_dp, tile, BLOCK).transpose(0, 2, 1, 3).reshape(n_tensor, tile, n_dp * BLOCK)
    return (new_master, new_moment, new_second, block_scales, forward_copy, transposed_copy)


def solution(mesh):
    spec = P("dp", "tensor")
    return jax.shard_map(
        body,
        mesh=mesh,
        in_specs=(spec,) * 4,
        out_specs=(spec, spec, spec, spec, P("dp", None), P(None, "dp", None)),
        check_vma=False,
    )
```

```python
import jax
import jax.numpy as jnp
from jax import lax
from jax.experimental import pallas as pl
from jax.experimental.pallas import tpu as pltpu
from jax.sharding import PartitionSpec as P

BLOCK = 128
beta_one = 0.9
beta_two = 0.95
learn_rate = 0.01
decay_rate = 0.1
epsilon = 1e-08
scale_eps = 1e-05
correct_one = 1.0 - 0.9**10
correct_two = 1.0 - 0.95**10


def step(master, grad, moment, second):
    new_moment = beta_one * moment + (1.0 - beta_one) * grad
    new_second = beta_two * second + (1.0 - beta_two) * grad * grad
    update = (
        new_moment / correct_one / (jnp.sqrt(new_second / correct_two) + epsilon)
        + decay_rate * master
    )
    return master - learn_rate * update, new_moment, new_second


def scaled_block(new_master):
    scale = jnp.max(jnp.abs(new_master)) + scale_eps
    return new_master / scale, scale


def z_visit(n):
    lead = n // 2 + 1
    far = [k for k in (0, 8, 2, 10, 1, 7, 15, 11, 3, 6, 14, 12, 4, 5, 13) if k < n and k != lead]
    rest = [k for k in range(n) if k != lead and k not in far]
    return [lead] + far + rest


def plane_visit(nx, ny, n_side):
    pairs = [((nx // 2 - i) % nx, (ny // 2 - j) % ny) for j in range(ny) for i in range(nx)]
    return [(x * (ny // n_side) + y // n_side, y % n_side) for x, y in pairs]


def flip_kernel(order, master_hbm, grad_hbm, moment_hbm, second_hbm, own_ref, held, sem):
    part = master_hbm.shape[0] // 4
    copies = [
        pltpu.make_async_copy(ref.at[pl.ds(k * part, part)], held.at[n, pl.ds(k * part, part)], sem)
        for k in range(4)
        for n, ref in enumerate((master_hbm, grad_hbm, moment_hbm, second_hbm))
    ]
    for n, copy in enumerate(copies):
        copy.start(priority=n % 2)
    for copy in copies:
        copy.wait()
    master_ref, grad_ref, moment_ref, second_ref = (held.at[n] for n in range(4))
    height, width = master_hbm.shape
    rows = width // len(order)
    for j in range(width // BLOCK):
        cols = slice(j * BLOCK, (j + 1) * BLOCK)
        new_master, _, _ = step(master_ref[:, cols], grad_ref[:, cols], moment_ref[:, cols], second_ref[:, cols])
        scaled, _ = scaled_block(new_master)
        flipped = scaled.T.astype(jnp.bfloat16)
        for k, owner in enumerate(order):
            if owner * rows // BLOCK == j:
                at = owner * rows - j * BLOCK
                own_ref[k * rows : (k + 1) * rows, :] = flipped[at : at + rows]
        own_ref[width + j * height : width + (j + 1) * height, :] = scaled.astype(jnp.bfloat16)


def repeat_kernel(load_ref, copies_ref):
    for k in range(copies_ref.shape[0]):
        copies_ref[k] = load_ref[...]


def spread_kernel(z_order, plane_order, load_ref, copies_ref):
    sides, slabs = load_ref.shape[:2]
    for side in range(sides):
        for s in range(slabs):
            for k, owner in enumerate(z_order):
                tile = load_ref[side, s, k]
                for n, (_, its) in enumerate(plane_order):
                    if its == side:
                        copies_ref[n, s, owner] = tile


def place_own(forward_order, flipped_order, flip, slabs_ref, forward_ref, flipped_ref, sem, work=None):
    core = (lax.axis_index("tensor") & 1) ^ flip
    width = forward_ref.shape[2] // slabs_ref.shape[0]

    def forward():
        copies = []
        for k, chip in enumerate(forward_order):
            for s in range(2):
                for j in range(width // BLOCK):
                    start = (2 * chip + s) * width + j * BLOCK
                    copies.append(
                        pltpu.make_async_copy(
                            slabs_ref.at[2 * k + s, j], forward_ref.at[:, :, start : start + BLOCK], sem
                        )
                    )
        return copies

    def flipped():
        copies = []
        for p, (chip, side) in enumerate(flipped_order):
            for s in range(2):
                copies.append(pltpu.make_async_copy(slabs_ref.at[p, s], flipped_ref.at[2 * chip + s, :, side], sem))
        return copies

    for which, copies in ((0, forward), (1, flipped)):

        @pl.when(core == which)
        def _(copies=copies):
            for n, copy in enumerate(copies()):
                copy.start(priority=n % 2)

    if work is not None:
        work()

    for which, copies in ((0, forward), (1, flipped)):

        @pl.when(core == which)
        def _(copies=copies):
            for copy in copies():
                copy.wait()


def finish_kernel(orders, slabs_ref, master_ref, grad_ref, moment_ref, second_ref, forward_ref, flipped_ref, out_master, out_moment, out_second, scale_ref, sem):
    def work():
        height, width = master_ref.shape
        for j in range(width // BLOCK):
            cols = slice(j * BLOCK, (j + 1) * BLOCK)
            new_master, new_moment, new_second = step(
                master_ref[:, cols], grad_ref[:, cols], moment_ref[:, cols], second_ref[:, cols]
            )
            out_master[:, cols] = new_master
            out_moment[:, cols] = new_moment
            out_second[:, cols] = new_second
            _, scale = scaled_block(new_master)
            scale_ref[0, j] = scale

    place_own(*orders, 0, slabs_ref, forward_ref, flipped_ref, sem, work)


def place_kernel(orders, slabs_ref, _, __, forward_ref, flipped_ref, sem):
    place_own(*orders, 1, slabs_ref, forward_ref, flipped_ref, sem)


def in_vmem(x):
    return pltpu.with_memory_space_constraint(x, pltpu.VMEM)


whole = pl.BlockSpec(memory_space=pltpu.VMEM)
hbm = pl.BlockSpec(memory_space=pl.ANY)


def body(master, grad, moment, second):
    height, width = master.shape
    n_dp, n_tensor = lax.axis_size("dp"), lax.axis_size("tensor")
    n_z, n_chip, n_side, tile = n_dp // 2, n_tensor // 2, 2, 8
    f32, bf16 = jnp.float32, jnp.bfloat16
    rows = height * width // BLOCK
    z_order = z_visit(n_z)
    chip_order = [(n_chip // 2 + 1 + k) % n_chip for k in range(n_chip)]
    plane_order = plane_visit(4, n_chip // 4 * n_side, n_side)
    orders = (chip_order, plane_order)
    own = pl.pallas_call(
        lambda *refs: flip_kernel(z_order, *refs),
        out_shape=pltpu.VMEM((2 * rows, BLOCK), bf16),
        in_specs=[hbm] * 4,
        out_specs=whole,
        scratch_shapes=[pltpu.VMEM((4, height, width), f32), pltpu.SemaphoreType.DMA],
        cost_estimate=pl.CostEstimate(flops=20 * height * width, bytes_accessed=16 * height * width, transcendentals=0),
        name="flip",
    )(master, grad, moment, second)
    both = lax.all_gather(own, "tensor", axis=0, axis_index_groups=[[2 * k, 2 * k + 1] for k in range(n_chip)])

    def forward_part(both):
        copies = pl.pallas_call(
            repeat_kernel,
            out_shape=pltpu.VMEM((n_chip, 2 * rows, BLOCK), bf16),
            in_specs=[whole],
            out_specs=whole,
            name="repeat",
        )(in_vmem(both[:, rows:].reshape(2 * rows, BLOCK)))
        groups = [[2 * k + c for k in chip_order] for c in range(2)]
        slabs = lax.all_to_all(copies, "tensor", 0, 0, tiled=True, axis_index_groups=groups)
        return slabs.reshape(n_tensor, width // BLOCK, height // tile, tile, BLOCK)

    def flipped_part(both):
        pieces = both[:, :rows].reshape(2, n_z, n_side, tile, BLOCK).transpose(1, 2, 0, 3, 4)
        groups = [[n_side * z + side for z in z_order] for side in range(n_side)]
        pieces = lax.all_to_all(pieces, "dp", 0, 0, tiled=True, axis_index_groups=groups)
        copies = pl.pallas_call(
            lambda *refs: spread_kernel(z_order, plane_order, *refs),
            out_shape=pltpu.VMEM((n_tensor, 2, n_z, tile, BLOCK), bf16),
            in_specs=[whole],
            out_specs=whole,
            name="spread",
        )(in_vmem(pieces.transpose(1, 2, 0, 3, 4)))
        groups = [
            [(n_side * z + side) * n_tensor + 2 * chip + c for chip, side in plane_order] for z in range(n_z) for c in range(2)
        ]
        slabs = lax.all_to_all(
            copies, ("dp", "tensor"), 0, 0, tiled=True, axis_index_groups=groups
        )
        return slabs.reshape(n_tensor, width // BLOCK, height // tile, tile, BLOCK)

    mine = lax.cond(lax.axis_index("tensor") % 2 == 1, flipped_part, forward_part, both)
    other = lax.ppermute(mine, "tensor", [(i, i ^ 1) for i in range(n_tensor)])
    same = jax.ShapeDtypeStruct((height, width), f32)
    outs = (
        jax.ShapeDtypeStruct((height // tile, tile, n_tensor * width), bf16),
        jax.ShapeDtypeStruct((n_tensor, n_z, n_side, tile, BLOCK), bf16),
    )
    forward_copy, transposed_copy, new_master, new_moment, new_second, block_scales = pl.pallas_call(
        lambda *refs: finish_kernel(orders, *refs),
        out_shape=(*outs, same, same, same, jax.ShapeDtypeStruct((1, width // BLOCK), f32)),
        in_specs=[whole] * 5,
        out_specs=(hbm, hbm, whole, whole, whole, pl.BlockSpec(memory_space=pltpu.SMEM)),
        scratch_shapes=[pltpu.SemaphoreType.DMA],
        cost_estimate=pl.CostEstimate(flops=20 * height * width, bytes_accessed=4 * mine.size, transcendentals=0),
        name="finish",
    )(in_vmem(mine), *(in_vmem(x) for x in (master, grad, moment, second)))
    forward_copy, transposed_copy = pl.pallas_call(
        lambda *refs: place_kernel(orders, *refs),
        out_shape=outs,
        in_specs=[whole, hbm, hbm],
        out_specs=(hbm, hbm),
        scratch_shapes=[pltpu.SemaphoreType.DMA],
        input_output_aliases={1: 0, 2: 1},
        cost_estimate=pl.CostEstimate(flops=0, bytes_accessed=4 * mine.size, transcendentals=0),
        name="place",
    )(in_vmem(other), forward_copy, transposed_copy)
    forward_copy = forward_copy.reshape(height, n_tensor * width)
    transposed_copy = transposed_copy.reshape(n_tensor, n_dp, tile, BLOCK).transpose(0, 2, 1, 3).reshape(n_tensor, tile, n_dp * BLOCK)
    return (new_master, new_moment, new_second, block_scales, forward_copy, transposed_copy)


def solution(mesh):
    spec = P("dp", "tensor")
    return jax.shard_map(
        body,
        mesh=mesh,
        in_specs=(spec,) * 4,
        out_specs=(spec, spec, spec, spec, P("dp", None), P(None, "dp", None)),
        check_vma=False,
    )
```

```python
import jax
import jax.numpy as jnp
from jax import lax
from jax.experimental import pallas as pl
from jax.experimental.pallas import tpu as pltpu
from jax.sharding import PartitionSpec as P

BLOCK = 128
beta_one = 0.9
beta_two = 0.95
learn_rate = 0.01
decay_rate = 0.1
epsilon = 1e-08
scale_eps = 1e-05
correct_one = 1.0 - 0.9**10
correct_two = 1.0 - 0.95**10


def step(master, grad, moment, second):
    new_moment = beta_one * moment + (1.0 - beta_one) * grad
    new_second = beta_two * second + (1.0 - beta_two) * grad * grad
    update = (
        new_moment / correct_one / (jnp.sqrt(new_second / correct_two) + epsilon)
        + decay_rate * master
    )
    return master - learn_rate * update, new_moment, new_second


def scaled_block(new_master):
    scale = jnp.max(jnp.abs(new_master)) + scale_eps
    return new_master / scale, scale


def z_visit(n):
    lead = n // 2 + 1
    far = [k for k in (0, 8, 2, 10, 1, 7, 15, 11, 3, 6, 14, 12, 4, 5, 13) if k < n and k != lead]
    rest = [k for k in range(n) if k != lead and k not in far]
    return [lead] + far + rest


def plane_visit(nx, ny, n_side):
    near = [((nx // 2 - i) % nx, (ny // 2 - j) % ny) for j in range(ny // 2) for i in range(nx)]
    pairs = [pair for x, y in near for pair in ((x, y), ((x + nx // 2) % nx, (y + ny // 2) % ny))]
    return [(x * (ny // n_side) + y // n_side, y % n_side) for x, y in pairs]


def flip_kernel(order, master_hbm, grad_hbm, moment_hbm, second_hbm, own_ref, held, sem):
    part = master_hbm.shape[0] // 4
    copies = [
        pltpu.make_async_copy(ref.at[pl.ds(k * part, part)], held.at[n, pl.ds(k * part, part)], sem)
        for k in range(4)
        for n, ref in enumerate((master_hbm, grad_hbm, moment_hbm, second_hbm))
    ]
    for n, copy in enumerate(copies):
        copy.start(priority=n % 2)
    for copy in copies:
        copy.wait()
    master_ref, grad_ref, moment_ref, second_ref = (held.at[n] for n in range(4))
    height, width = master_hbm.shape
    rows = width // len(order)
    for j in range(width // BLOCK):
        cols = slice(j * BLOCK, (j + 1) * BLOCK)
        new_master, _, _ = step(master_ref[:, cols], grad_ref[:, cols], moment_ref[:, cols], second_ref[:, cols])
        scaled, _ = scaled_block(new_master)
        flipped = scaled.T.astype(jnp.bfloat16)
        for k, owner in enumerate(order):
            if owner * rows // BLOCK == j:
                at = owner * rows - j * BLOCK
                own_ref[k * rows : (k + 1) * rows, :] = flipped[at : at + rows]
        own_ref[width + j * height : width + (j + 1) * height, :] = scaled.astype(jnp.bfloat16)


def repeat_kernel(load_ref, copies_ref):
    for k in range(copies_ref.shape[0]):
        copies_ref[k] = load_ref[...]


def spread_kernel(z_order, plane_order, load_ref, copies_ref):
    sides, slabs = load_ref.shape[:2]
    for side in range(sides):
        for s in range(slabs):
            for k, owner in enumerate(z_order):
                tile = load_ref[side, s, k]
                for n, (_, its) in enumerate(plane_order):
                    if its == side:
                        copies_ref[n, s, owner] = tile


def place_own(forward_order, flipped_order, flip, slabs_ref, forward_ref, flipped_ref, sem, work=None):
    core = (lax.axis_index("tensor") & 1) ^ flip
    width = forward_ref.shape[2] // slabs_ref.shape[0]

    def forward():
        copies = []
        for k, chip in enumerate(forward_order):
            for s in range(2):
                for j in range(width // BLOCK):
                    start = (2 * chip + s) * width + j * BLOCK
                    copies.append(
                        pltpu.make_async_copy(
                            slabs_ref.at[2 * k + s, j], forward_ref.at[:, :, start : start + BLOCK], sem
                        )
                    )
        return copies

    def flipped():
        copies = []
        for p, (chip, side) in enumerate(flipped_order):
            for s in range(2):
                copies.append(pltpu.make_async_copy(slabs_ref.at[p, s], flipped_ref.at[2 * chip + s, :, side], sem))
        return copies

    for which, copies in ((0, forward), (1, flipped)):

        @pl.when(core == which)
        def _(copies=copies):
            for n, copy in enumerate(copies()):
                copy.start(priority=n % 2)

    if work is not None:
        work()

    for which, copies in ((0, forward), (1, flipped)):

        @pl.when(core == which)
        def _(copies=copies):
            for copy in copies():
                copy.wait()


def finish_kernel(orders, slabs_ref, master_ref, grad_ref, moment_ref, second_ref, forward_ref, flipped_ref, out_master, out_moment, out_second, scale_ref, sem):
    def work():
        height, width = master_ref.shape
        for j in range(width // BLOCK):
            cols = slice(j * BLOCK, (j + 1) * BLOCK)
            new_master, new_moment, new_second = step(
                master_ref[:, cols], grad_ref[:, cols], moment_ref[:, cols], second_ref[:, cols]
            )
            out_master[:, cols] = new_master
            out_moment[:, cols] = new_moment
            out_second[:, cols] = new_second
            _, scale = scaled_block(new_master)
            scale_ref[0, j] = scale

    place_own(*orders, 0, slabs_ref, forward_ref, flipped_ref, sem, work)


def place_kernel(orders, slabs_ref, _, __, forward_ref, flipped_ref, sem):
    place_own(*orders, 1, slabs_ref, forward_ref, flipped_ref, sem)


def in_vmem(x):
    return pltpu.with_memory_space_constraint(x, pltpu.VMEM)


whole = pl.BlockSpec(memory_space=pltpu.VMEM)
hbm = pl.BlockSpec(memory_space=pl.ANY)


def body(master, grad, moment, second):
    height, width = master.shape
    n_dp, n_tensor = lax.axis_size("dp"), lax.axis_size("tensor")
    n_z, n_chip, n_side, tile = n_dp // 2, n_tensor // 2, 2, 8
    f32, bf16 = jnp.float32, jnp.bfloat16
    rows = height * width // BLOCK
    z_order = z_visit(n_z)
    chip_order = [(n_chip // 2 + 1 + k) % n_chip for k in range(n_chip)]
    plane_order = plane_visit(4, n_chip // 4 * n_side, n_side)
    orders = (chip_order, plane_order)
    own = pl.pallas_call(
        lambda *refs: flip_kernel(z_order, *refs),
        out_shape=pltpu.VMEM((2 * rows, BLOCK), bf16),
        in_specs=[hbm] * 4,
        out_specs=whole,
        scratch_shapes=[pltpu.VMEM((4, height, width), f32), pltpu.SemaphoreType.DMA],
        cost_estimate=pl.CostEstimate(flops=20 * height * width, bytes_accessed=16 * height * width, transcendentals=0),
        name="flip",
    )(master, grad, moment, second)
    both = lax.all_gather(own, "tensor", axis=0, axis_index_groups=[[2 * k, 2 * k + 1] for k in range(n_chip)])

    def forward_part(both):
        copies = pl.pallas_call(
            repeat_kernel,
            out_shape=pltpu.VMEM((n_chip, 2 * rows, BLOCK), bf16),
            in_specs=[whole],
            out_specs=whole,
            name="repeat",
        )(in_vmem(both[:, rows:].reshape(2 * rows, BLOCK)))
        groups = [[2 * k + c for k in chip_order] for c in range(2)]
        slabs = lax.all_to_all(copies, "tensor", 0, 0, tiled=True, axis_index_groups=groups)
        return slabs.reshape(n_tensor, width // BLOCK, height // tile, tile, BLOCK)

    def flipped_part(both):
        pieces = both[:, :rows].reshape(2, n_z, n_side, tile, BLOCK).transpose(1, 2, 0, 3, 4)
        groups = [[n_side * z + side for z in z_order] for side in range(n_side)]
        pieces = lax.all_to_all(pieces, "dp", 0, 0, tiled=True, axis_index_groups=groups)
        copies = pl.pallas_call(
            lambda *refs: spread_kernel(z_order, plane_order, *refs),
            out_shape=pltpu.VMEM((n_tensor, 2, n_z, tile, BLOCK), bf16),
            in_specs=[whole],
            out_specs=whole,
            name="spread",
        )(in_vmem(pieces.transpose(1, 2, 0, 3, 4)))
        groups = [
            [(n_side * z + side) * n_tensor + 2 * chip + c for chip, side in plane_order] for z in range(n_z) for c in range(2)
        ]
        slabs = lax.all_to_all(
            copies, ("dp", "tensor"), 0, 0, tiled=True, axis_index_groups=groups
        )
        return slabs.reshape(n_tensor, width // BLOCK, height // tile, tile, BLOCK)

    mine = lax.cond(lax.axis_index("tensor") % 2 == 1, flipped_part, forward_part, both)
    other = lax.ppermute(mine, "tensor", [(i, i ^ 1) for i in range(n_tensor)])
    same = jax.ShapeDtypeStruct((height, width), f32)
    outs = (
        jax.ShapeDtypeStruct((height // tile, tile, n_tensor * width), bf16),
        jax.ShapeDtypeStruct((n_tensor, n_z, n_side, tile, BLOCK), bf16),
    )
    forward_copy, transposed_copy, new_master, new_moment, new_second, block_scales = pl.pallas_call(
        lambda *refs: finish_kernel(orders, *refs),
        out_shape=(*outs, same, same, same, jax.ShapeDtypeStruct((1, width // BLOCK), f32)),
        in_specs=[whole] * 5,
        out_specs=(hbm, hbm, whole, whole, whole, pl.BlockSpec(memory_space=pltpu.SMEM)),
        scratch_shapes=[pltpu.SemaphoreType.DMA],
        cost_estimate=pl.CostEstimate(flops=20 * height * width, bytes_accessed=4 * mine.size, transcendentals=0),
        name="finish",
    )(in_vmem(mine), *(in_vmem(x) for x in (master, grad, moment, second)))
    forward_copy, transposed_copy = pl.pallas_call(
        lambda *refs: place_kernel(orders, *refs),
        out_shape=outs,
        in_specs=[whole, hbm, hbm],
        out_specs=(hbm, hbm),
        scratch_shapes=[pltpu.SemaphoreType.DMA],
        input_output_aliases={1: 0, 2: 1},
        cost_estimate=pl.CostEstimate(flops=0, bytes_accessed=4 * mine.size, transcendentals=0),
        name="place",
    )(in_vmem(other), forward_copy, transposed_copy)
    forward_copy = forward_copy.reshape(height, n_tensor * width)
    transposed_copy = transposed_copy.reshape(n_tensor, n_dp, tile, BLOCK).transpose(0, 2, 1, 3).reshape(n_tensor, tile, n_dp * BLOCK)
    return (new_master, new_moment, new_second, block_scales, forward_copy, transposed_copy)


def solution(mesh):
    spec = P("dp", "tensor")
    return jax.shard_map(
        body,
        mesh=mesh,
        in_specs=(spec,) * 4,
        out_specs=(spec, spec, spec, spec, P("dp", None), P(None, "dp", None)),
        check_vma=False,
    )
```
